32 devices in a mesh: groups: 2 (over y), space: 16 (over z, x, core).
Axes of the slice: x: 2, y: 2, z: 4, core: 2. Of those that a mesh axis runs over, the one named last changes fastest.
Arguments:
- coarse_input: bfloat16 [256, 16, 256], P('groups', 'space'), parts along dimension 0, may hold values from -6 to 6
- skip: bfloat16 [128, 32, 1024], P('groups', None, 'space'), parts along dimension 0, may hold values from -6 to 6
- cotangent: bfloat16 [128, 32, 1024], P('groups', 'space'), parts along dimension 0, may hold values from -6 to 6
- w_up: bfloat16 [8, 64, 128], replicated, may hold values from -0.5 to 0.5
- w_conv: bfloat16 [27, 64, 128], replicated, may hold values from -0.109375 to 0.109375
Outputs:
- activation: bfloat16 [128, 32, 1024], P('groups', 'space'), parts along dimension 0
- grad_input: bfloat16 [256, 16, 256], P('groups', 'space'), parts along dimension 0
- grad_skip: bfloat16 [128, 32, 1024], P('groups', None, 'space'), parts along dimension 0
- grad_w_up: float32 [16, 64, 128], P('groups'), parts along dimension 0
- grad_w_conv: float32 [54, 64, 128], P('groups'), parts along dimension 0
The draws below stay inside these ranges and needn't reach their ends.
There are 2 independent parts, one for each index of `groups`. The reference program is written for one: setup_inputs(seed, part) draws one part's arguments, and reference() takes and returns one part's arrays. A program takes and returns all parts, laid end to end along the dimension named above; an argument that names none is the same for every part. Nothing has to cross between parts.
All inputs are finite; a program needn't handle non-finite values.
Results may differ from the reference program's by a relative error of at most 0.012.
Values may be sent and summed in bfloat16 or wider, within the bound.
A program may use at most 64 MiB of HBM per device.

```python
import math
import jax
import jax.numpy as jnp
from jax import lax

CIN = 128
CUP = 64
CSK = 64
COUT = 64
CCAT = 128
H = 8
W = 128
CDEP = 16
FD = 32


def steps_of(rng, extent, split, low, top_value):
    level = 1.0
    for dim, parts in split:
        draws = jax.random.uniform(jax.random.fold_in(jax.random.fold_in(rng, 6), dim), (parts,), jnp.float32, low / len(split), top_value / len(split))
        level = level * jnp.repeat(jnp.exp(draws), extent[dim] // parts).reshape((-1,) + (1,) * (len(extent) - 1 - dim))
    return level


def normal_values(rng, shape, deviation, most, shards=(), dtype=jnp.bfloat16):
    result = jax.random.normal(rng, shape, jnp.float32) * deviation
    if len(shards) > 0:
        result = steps_of(rng, shape, shards, -0.22, 0.18) * result
    return jnp.clip(result, min=-most, max=most).astype(dtype)


def setup_inputs(seed: int = 0, part: int = 0) -> dict:
    key_list = jax.random.split(jax.random.key(seed), 6)
    part_splits = jax.random.split(jax.random.fold_in(key_list[5], part), 6)
    return {
        "coarse_input": normal_values(part_splits[0], (CIN, CDEP, (H // 2) * (W // 2)), 1.0, 6.0, ((1, 16),)),
        "skip": normal_values(part_splits[1], (CSK, FD, H * W), 1.0, 6.0, ((2, 16),)),
        "cotangent": normal_values(part_splits[2], (COUT, FD, H * W), 1.0, 6.0, ((1, 16),)),
        "w_up": normal_values(key_list[3], (8, CUP, CIN), CIN ** -0.5, 0.5),
        "w_conv": normal_values(key_list[4], (27, COUT, CCAT), (27 * CCAT) ** -0.5, 0.109375),
    }


def upsample_ref(coarse, w_up, height, width):
    channels = coarse.shape[0]
    planes = coarse.shape[1]
    outputs = w_up.shape[1]
    terms = jnp.dot(w_up.reshape(8 * outputs, channels), coarse.reshape(channels, -1), preferred_element_type=jnp.float32)
    terms = terms.reshape(2, 2, 2, outputs, planes, height // 2, width // 2)
    terms = terms.transpose(3, 4, 0, 5, 1, 6, 2)
    return terms.reshape(outputs, 2 * planes, height, width).astype(jnp.bfloat16)

def pad_all(volume):
    return jnp.pad(volume, ((0, 0), (1, 1), (1, 1), (1, 1)))

def reference(coarse_input, skip, cotangent, w_up, w_conv):
    planes = FD
    height = H
    width = W
    upsampled = upsample_ref(coarse_input, w_up, height, width)
    joined = jnp.concatenate([upsampled, skip.reshape(CSK, planes, height, width)], 0)
    joined_pad = pad_all(joined)
    pre = jnp.zeros((COUT, planes * height * width), jnp.float32)
    for depth_tap in range(3):
        for row_tap in range(3):
            for col_tap in range(3):
                window = joined_pad[:, depth_tap:depth_tap + planes, row_tap:row_tap + height, col_tap:col_tap + width].reshape(CCAT, -1)
                pre = pre + jnp.dot(w_conv[9 * depth_tap + 3 * row_tap + col_tap], window, preferred_element_type=jnp.float32)
    gate = jax.nn.sigmoid(pre)
    activation = (pre * gate).astype(jnp.bfloat16)
    grad_pre = (cotangent.reshape(COUT, -1).astype(jnp.float32) * gate * (1.0 + pre * (1.0 - gate))).astype(jnp.bfloat16)
    grad_pad = pad_all(grad_pre.reshape(COUT, planes, height, width))
    grad_joined = jnp.zeros((CCAT, planes * height * width), jnp.float32)
    weight_terms = []
    flat_grad = grad_pre
    for depth_tap in range(3):
        for row_tap in range(3):
            for col_tap in range(3):
                tap = 9 * depth_tap + 3 * row_tap + col_tap
                window = grad_pad[:, 2 - depth_tap:2 - depth_tap + planes, 2 - row_tap:2 - row_tap + height, 2 - col_tap:2 - col_tap + width].reshape(COUT, -1)
                grad_joined = grad_joined + lax.dot_general(w_conv[tap], window, (((0,), (0,)), ((), ())), preferred_element_type=jnp.float32)
                source = joined_pad[:, depth_tap:depth_tap + planes, row_tap:row_tap + height, col_tap:col_tap + width].reshape(CCAT, -1)
                weight_terms.append(lax.dot_general(flat_grad, source, (((1,), (1,)), ((), ())), preferred_element_type=jnp.float32))
    grad_up = grad_joined[:CUP].astype(jnp.bfloat16)
    grad_skip = grad_joined[CUP:].astype(jnp.bfloat16).reshape(CSK, planes, height * width)
    arranged = grad_up.reshape(CUP, planes // 2, 2, height // 2, 2, width // 2, 2).transpose(2, 4, 6, 0, 1, 3, 5).reshape(8 * CUP, -1)
    grad_input = lax.dot_general(w_up.reshape(8 * CUP, CIN), arranged, (((0,), (0,)), ((), ())), preferred_element_type=jnp.float32)
    grad_input = grad_input.astype(jnp.bfloat16).reshape(CIN, planes // 2, -1)
    scale = 1.0 / math.sqrt(FD * H * W)
    grad_w_up = lax.dot_general(arranged, coarse_input.reshape(CIN, -1), (((1,), (1,)), ((), ())), preferred_element_type=jnp.float32)
    grad_w_up = grad_w_up.reshape(8, CUP, CIN) * scale
    grad_w_conv = jnp.stack(weight_terms, 0) * scale
    return (activation.reshape(COUT, planes, height * width), grad_input, grad_skip, grad_w_up, grad_w_conv)
```

```python
import functools
import math

import jax
import jax.numpy as jnp
from jax import lax
from jax.experimental import pallas as pl
from jax.experimental.pallas import tpu as pltpu
from jax.sharding import PartitionSpec as P

W = 128


def padded_2(value, sides, width):
    for axis, dim in sides:
        peers, length = (lax.axis_size(axis), value.shape[dim])
        up = [(i, (i + 1) % peers) for i in range(peers - 1)]
        down = [(j, i) for i, j in up]
        last = lax.slice_in_dim(value, length - width, length, axis=dim)
        leading = lax.slice_in_dim(value, 0, width, axis=dim)
        before = lax.ppermute(last, axis, up)
        after = lax.ppermute(leading, axis, down)
        value = jnp.concatenate([before, value, after], axis=dim)
    return value


def upsample(coarse, w_up, height, width):
    channels = coarse.shape[0]
    planes = coarse.shape[1]
    outputs = w_up.shape[1]
    terms = jnp.dot(
        w_up.reshape(8 * outputs, channels),
        coarse.reshape(channels, -1),
        preferred_element_type=jnp.float32,
    )
    terms = terms.reshape(2, 2, 2, outputs, planes, height // 2, width // 2)
    terms = terms.transpose(3, 4, 0, 5, 1, 6, 2)
    return terms.reshape(outputs, 2 * planes, height, width).astype(jnp.bfloat16)


def pad_sides(volume):
    return jnp.pad(volume, ((0, 0), (0, 0), (1, 1), (1, 1)))


def conv_forward(padded, w_conv, planes, height, width):
    channels = padded.shape[0]
    total = jnp.zeros((w_conv.shape[1], planes * height * width), jnp.float32)
    for depth_tap in range(3):
        for row_tap in range(3):
            for col_tap in range(3):
                window = padded[
                    :,
                    depth_tap : depth_tap + planes,
                    row_tap : row_tap + height,
                    col_tap : col_tap + width,
                ].reshape(channels, -1)
                total = total + jnp.dot(
                    w_conv[9 * depth_tap + 3 * row_tap + col_tap],
                    window,
                    preferred_element_type=jnp.float32,
                )
    return total


def conv_input_grad(padded, w_conv, planes, height, width):
    channels = padded.shape[0]
    total = jnp.zeros((w_conv.shape[2], planes * height * width), jnp.float32)
    for depth_tap in range(3):
        for row_tap in range(3):
            for col_tap in range(3):
                window = padded[
                    :,
                    2 - depth_tap : 2 - depth_tap + planes,
                    2 - row_tap : 2 - row_tap + height,
                    2 - col_tap : 2 - col_tap + width,
                ].reshape(channels, -1)
                total = total + lax.dot_general(
                    w_conv[9 * depth_tap + 3 * row_tap + col_tap],
                    window,
                    (((0,), (0,)), ((), ())),
                    preferred_element_type=jnp.float32,
                )
    return total


def conv_weight_grad(padded, grad_flat, planes, height, width):
    channels = padded.shape[0]
    results = []
    for depth_tap in range(3):
        for row_tap in range(3):
            for col_tap in range(3):
                window = padded[
                    :,
                    depth_tap : depth_tap + planes,
                    row_tap : row_tap + height,
                    col_tap : col_tap + width,
                ].reshape(channels, -1)
                results.append(
                    lax.dot_general(
                        grad_flat,
                        window,
                        (((1,), (1,)), ((), ())),
                        preferred_element_type=jnp.float32,
                    )
                )
    return jnp.stack(results, 0)


def local(coarse_input, skip, cotangent, w_up, w_conv):
    devices = lax.axis_size("space")
    channels_in = coarse_input.shape[0]
    coarse_planes = coarse_input.shape[1]
    up_channels = w_up.shape[1]
    skip_channels = skip.shape[0]
    out_channels = cotangent.shape[0]
    planes = cotangent.shape[1]
    cells = cotangent.shape[2]
    width = W
    height = cells // width
    joined_channels = up_channels + skip_channels
    skip_local = lax.all_to_all(skip, "space", split_axis=1, concat_axis=2, tiled=True)
    upsampled = upsample(coarse_input, w_up, height, width)
    joined = jnp.concatenate([upsampled.reshape(up_channels, planes, cells), skip_local], 0)
    joined_ext = padded_2(joined, (("space", 1),), 1)
    joined_pad = pad_sides(joined_ext.reshape(joined_channels, planes + 2, height, width))
    pre = conv_forward(joined_pad, w_conv, planes, height, width)
    gate = jax.nn.sigmoid(pre)
    activation = (pre * gate).astype(jnp.bfloat16).reshape(out_channels, planes, cells)
    grad_pre = (
        cotangent.reshape(out_channels, -1).astype(jnp.float32) * gate * (1.0 + pre * (1.0 - gate))
    ).astype(jnp.bfloat16)
    grad_ext = padded_2(grad_pre.reshape(out_channels, planes, cells), (("space", 1),), 1)
    grad_pad = pad_sides(grad_ext.reshape(out_channels, planes + 2, height, width))
    grad_joined = conv_input_grad(grad_pad, w_conv, planes, height, width)
    grad_up = grad_joined[:up_channels].astype(jnp.bfloat16)
    skip_part = grad_joined[up_channels:].astype(jnp.bfloat16).reshape(skip_channels, planes, cells)
    grad_skip = lax.all_to_all(skip_part, "space", split_axis=2, concat_axis=1, tiled=True)
    arranged = (
        grad_up.reshape(up_channels, coarse_planes, 2, height // 2, 2, width // 2, 2)
        .transpose(2, 4, 6, 0, 1, 3, 5)
        .reshape(8 * up_channels, -1)
    )
    flat_up = w_up.reshape(8 * up_channels, channels_in)
    grad_input = lax.dot_general(
        flat_up, arranged, (((0,), (0,)), ((), ())), preferred_element_type=jnp.float32
    )
    grad_input = grad_input.astype(jnp.bfloat16).reshape(channels_in, coarse_planes, -1)
    local_up = lax.dot_general(
        arranged,
        coarse_input.reshape(channels_in, -1),
        (((1,), (1,)), ((), ())),
        preferred_element_type=jnp.float32,
    )
    local_up = local_up.reshape(8, up_channels, channels_in)
    local_conv = conv_weight_grad(joined_pad, grad_pre, planes, height, width)
    scale = 1.0 / math.sqrt(devices * planes * cells)
    summed_up, summed_conv = lax.psum((local_up * scale, local_conv * scale), "space")
    return (activation, grad_input, grad_skip, summed_up, summed_conv)


H = 8
ROW = (H + 2) * W
PLANE = H * W
PART = 144
F32 = jnp.float32
BF16 = jnp.bfloat16


def remote(src, dst, send, recv, peer):
    return pltpu.make_async_remote_copy(
        src_ref=src,
        dst_ref=dst,
        send_sem=send,
        recv_sem=recv,
        device_id={"space": peer},
        device_id_type=pl.DeviceIdType.MESH,
    )


def mm(a, b):
    return jnp.dot(a, b, preferred_element_type=F32)


def mm_nt(a, b):
    return lax.dot_general(a, b, (((1,), (1,)), ((), ())), preferred_element_type=F32)


def mm_tn(a, b):
    return lax.dot_general(a, b, (((0,), (0,)), ((), ())), preferred_element_type=F32)


def fused_kernel(
    n, scale,
    coarse, skip, cot, w_up, w_conv,
    act_out, gin_out, gskip_out, gup_out, gconv_out,
    w_f, w_u, c_halo, s_got, s_planes, x_buf, g_planes, g_buf, t_send, t_got,
    part, pair, total, got, full, send, recv,
):
    me = lax.axis_index("space")
    chips = n // 2
    core = lax.rem(me, 2)
    chip = lax.div(me, 2)
    partner = me + 1 - 2 * core
    half = chips * PART
    mine = pl.multiple_of(core * half, 16)
    other = pl.multiple_of((1 - core) * half, 16)
    lane = lax.broadcasted_iota(jnp.int32, (64, W), 1)
    low = lane < 64

    c_halo[...] = jnp.zeros_like(c_halo)
    s_planes[...] = jnp.zeros_like(s_planes)
    g_planes[...] = jnp.zeros_like(g_planes)

    barrier = pltpu.get_barrier_semaphore()

    @pl.loop(1, n)
    def _(k):
        pl.semaphore_signal(
            barrier, inc=1, device_id={"space": lax.rem(me + k, n)},
            device_id_type=pl.DeviceIdType.MESH,
        )

    pl.semaphore_wait(barrier, n - 1)

    def skip_copy(k):
        peer = lax.rem(me + k, n)
        return remote(skip.at[peer], s_got.at[me], send.at[0, k], recv.at[0, k], peer)

    @pl.loop(1, n)
    def _(k):
        skip_copy(k).start()

    def halo(src_up, src_down, dst_prev, dst_next, index):
        up = remote(src_up, dst_prev, send.at[1, index], recv.at[1, index], me + 1)
        down = remote(src_down, dst_next, send.at[1, index + 1], recv.at[1, index + 1], me - 1)

        def start():
            pl.when(me < n - 1)(up.start)
            pl.when(me > 0)(down.start)

        def wait():
            pl.when(me < n - 1)(up.wait_send)
            pl.when(me > 0)(down.wait_send)
            pl.when(me > 0)(up.wait_recv)
            pl.when(me < n - 1)(down.wait_recv)

        return start, wait

    c_start, c_wait = halo(coarse, coarse, c_halo.at[0], c_halo.at[1], 0)
    c_start()

    x_buf[...] = jnp.zeros_like(x_buf)
    g_buf[...] = jnp.zeros_like(g_buf)
    for a in range(3):
        for b in range(3):
            for c in range(3):
                ab = 3 * a + b
                w_f[64 * c : 64 * c + 64, 128 * ab : 128 * ab + 128] = w_conv[9 * a + 3 * b + c]
    for ij in range(4):
        for k in range(2):
            w_u[64 * ij : 64 * ij + 64, 128 * k : 128 * k + 128] = w_up[2 * ij + k]

    source = lax.broadcasted_iota(jnp.int32, (W, W), 0)
    target = lax.broadcasted_iota(jnp.int32, (W, W), 1)

    def spread(h2, k):
        return jnp.where(target == 2 * (source - 64 * h2) + k, 1.0, 0.0).astype(BF16)

    spreads = [[jnp.where((source >= 64 * h2) & (source < 64 * h2 + 64), spread(h2, k), 0) for k in range(2)] for h2 in range(2)]

    def expand(value):
        return jnp.concatenate(
            [
                jnp.concatenate(
                    [mm(value[:, 128 * (h // 2) : 128 * (h // 2) + 128], spreads[h % 2][k]) for h in range(H // 2)],
                    axis=1,
                )
                for k in range(2)
            ],
            axis=0,
        ).astype(BF16)

    def place(value, plane, j):
        for h in range(H // 2):
            at = plane * ROW + (2 * h + j + 1) * W
            x_buf[0:64, at : at + W] = value[:, h * W : (h + 1) * W].astype(BF16)

    c_exp = expand(coarse[...])
    up = mm(w_u[...], c_exp)
    for ij in range(4):
        place(up[64 * ij : 64 * ij + 64], 1 + ij // 2, ij % 2)
    c_wait()
    up = mm(w_u[128:256], expand(c_halo[0]))
    place(up[0:64], 0, 0)
    place(up[64:128], 0, 1)
    up = mm(w_u[0:128], expand(c_halo[1]))
    place(up[0:64], 3, 0)
    place(up[64:128], 3, 1)

    @pl.loop(1, n)
    def _(k):
        skip_copy(k).wait()

    s_got[me] = skip[me]
    for h in range(H):
        left = s_got[2 * h].astype(F32)
        right = s_got[2 * h + 1].astype(F32)
        first = jnp.where(low, left, pltpu.roll(right, 64, 1)).astype(BF16)
        second = jnp.where(low, pltpu.roll(left, 64, 1), right).astype(BF16)
        s_planes[1, :, h * W : (h + 1) * W] = first
        s_planes[2, :, h * W : (h + 1) * W] = second
    s_start, s_wait = halo(s_planes.at[2], s_planes.at[1], s_planes.at[0], s_planes.at[3], 2)
    s_start()
    for plane in (1, 2):
        x_buf[64:128, plane * ROW + W : plane * ROW + W + PLANE] = s_planes[plane]
    s_wait()
    for plane in (0, 3):
        x_buf[64:128, plane * ROW + W : plane * ROW + W + PLANE] = s_planes[plane]

    def windows(buf, plane, sign):
        parts = []
        for a in range(3):
            for b in range(3):
                at = (plane + 1 + sign * (a - 1)) * ROW + W + sign * (b - 1) * W
                parts.append(buf[:, at : at + PLANE])
        return jnp.concatenate(parts, axis=0)

    for plane in range(2):
        y = mm(w_f[...], windows(x_buf, plane, 1))
        for h in range(H):
            at = slice(h * W, (h + 1) * W)
            full_at = slice(plane * PLANE + h * W, plane * PLANE + (h + 1) * W)
            pre = (
                y[64:128, at]
                + jnp.where(lane > 0, pltpu.roll(y[0:64, at], 1, 1), 0.0)
                + jnp.where(lane < W - 1, pltpu.roll(y[128:192, at], W - 1, 1), 0.0)
            )
            gate = 1.0 / (1.0 + jnp.exp(-pre))
            act_out[:, full_at] = (pre * gate).astype(BF16)
            grad = cot[:, full_at].astype(F32) * gate * (1.0 + pre * (1.0 - gate))
            g_planes[plane + 1, :, at] = grad.astype(BF16)

    g_start, g_wait = halo(g_planes.at[2], g_planes.at[1], g_planes.at[0], g_planes.at[3], 4)
    g_start()

    def fill(plane):
        for h in range(H):
            value = g_planes[plane, :, h * W : (h + 1) * W]
            wide = value.astype(F32)
            at = plane * ROW + (h + 1) * W
            g_buf[64:128, at : at + W] = value
            g_buf[0:64, at : at + W] = jnp.where(lane < W - 1, pltpu.roll(wide, W - 1, 1), 0.0).astype(BF16)
            g_buf[128:192, at : at + W] = jnp.where(lane > 0, pltpu.roll(wide, 1, 1), 0.0).astype(BF16)

    fill(1)
    fill(2)

    d_conv = None
    for plane in range(2):
        at = (plane + 1) * ROW + W
        term = mm_nt(g_buf[:, at : at + PLANE], windows(x_buf, plane, 1))
        d_conv = term if d_conv is None else d_conv + term
    for a in range(3):
        for b in range(3):
            for c in range(3):
                ab = 3 * a + b
                row = 64 * (9 * a + 3 * b + c)
                part[row : row + 64, :] = d_conv[64 * c : 64 * c + 64, 128 * ab : 128 * ab + 128].astype(BF16)

    g_wait()
    fill(0)
    fill(3)
    w_b = w_conv[...].reshape(27 * 64, 128)
    joined = [mm_tn(w_b, windows(g_buf, plane, -1)) for plane in range(2)]
    for h in range(H):
        at = slice(h * W, (h + 1) * W)
        first, second = joined[0][64:128, at], joined[1][64:128, at]
        t_send[2 * h] = jnp.where(low, first, pltpu.roll(second, 64, 1)).astype(BF16)
        t_send[2 * h + 1] = jnp.where(low, pltpu.roll(first, 64, 1), second).astype(BF16)

    def grad_copy(k):
        peer = lax.rem(me + k, n)
        return remote(t_send.at[peer], t_got.at[me], send.at[2, k], recv.at[2, k], peer)

    @pl.loop(1, n)
    def _(k):
        grad_copy(k).start()

    g_up = jnp.concatenate(
        [
            jnp.concatenate([joined[ij // 2][0:64, (2 * h + ij % 2) * W : (2 * h + ij % 2 + 1) * W] for h in range(H // 2)], axis=1)
            for ij in range(4)
        ],
        axis=0,
    ).astype(BF16)
    d_up = mm_nt(g_up, c_exp)
    for ij in range(4):
        for k in range(2):
            row = 64 * (27 + 2 * ij + k)
            part[row : row + 64, :] = d_up[64 * ij : 64 * ij + 64, 128 * k : 128 * k + 128].astype(BF16)
    part[35 * 64 :, :] = jnp.zeros((n * PART - 35 * 64, 128), BF16)

    swap = remote(part.at[pl.ds(other, half)], pair, send.at[5, 0], recv.at[5, 0], partner)
    swap.start()

    squeeze = jnp.where(source == 2 * lax.rem(target, 64) + lax.div(target, 64), 1.0, 0.0).astype(BF16)
    wide_low = lax.broadcasted_iota(jnp.int32, (128, W), 1) < 64
    packed = [mm(g_up[:, h * W : (h + 1) * W], squeeze).astype(BF16) for h in range(H // 2)]
    both = mm_tn(w_u[...], jnp.concatenate(packed, axis=1))
    for h in range(0, H // 2, 2):
        z0 = both[0:128, h * W : (h + 1) * W] + pltpu.roll(both[128:256, h * W : (h + 1) * W], 64, 1)
        z1 = pltpu.roll(both[0:128, (h + 1) * W : (h + 2) * W], 64, 1) + both[128:256, (h + 1) * W : (h + 2) * W]
        gin_out[:, h * 64 : h * 64 + 128] = jnp.where(wide_low, z0, z1).astype(BF16)

    swap.wait()
    total[...] = (part[pl.ds(mine, half), :].astype(F32) + pair[...].astype(F32)).astype(BF16)

    def chunk(index):
        return pl.ds(pl.multiple_of(index * PART, 16), PART)

    def reduce_copy(k):
        peer = lax.rem(chip + k, chips)
        return remote(total.at[chunk(peer)], got.at[k], send.at[3, k], recv.at[3, k], 2 * peer + core)

    @pl.loop(1, chips)
    def _(k):
        reduce_copy(k).start()

    @pl.loop(1, chips)
    def _(k):
        reduce_copy(k).wait()

    summed = total[chunk(chip), :].astype(F32)
    for k in range(1, chips):
        summed = summed + got[k].astype(F32)
    own = pl.ds(pl.multiple_of(core * half + chip * PART, 16), PART)
    full[own, :] = (summed * scale).astype(BF16)

    def gather_copy(k):
        peer = lax.rem(chip + k, chips)
        return remote(full.at[own], full.at[own], send.at[4, k], recv.at[4, k], 2 * peer + core)

    @pl.loop(1, chips)
    def _(k):
        gather_copy(k).start()

    @pl.loop(1, n)
    def _(k):
        grad_copy(k).wait()

    t_got[me] = t_send[me]
    gskip_out[...] = t_got[...]

    @pl.loop(1, chips)
    def _(k):
        gather_copy(k).wait()

    back = remote(full.at[pl.ds(mine, half)], full.at[pl.ds(mine, half)], send.at[5, 1], recv.at[5, 1], partner)
    back.start()
    back.wait()
    for tap in range(27):
        gconv_out[tap] = full[64 * tap : 64 * tap + 64, :].astype(F32)
    for tap in range(8):
        gup_out[tap] = full[64 * (27 + tap) : 64 * (28 + tap), :].astype(F32)


def fused_local(coarse_input, skip, cotangent, w_up, w_conv):
    n = lax.axis_size("space")
    planes = cotangent.shape[1]
    cells = cotangent.shape[2]
    skip_rows = skip.reshape(64, n, 128).transpose(1, 0, 2)
    scale = 1.0 / math.sqrt(n * planes * cells)
    shape = jax.ShapeDtypeStruct
    vmem = pl.BlockSpec(memory_space=pltpu.VMEM)
    half = n // 2 * PART
    act, grad_in, grad_skip, d_up, d_conv = pl.pallas_call(
        functools.partial(fused_kernel, n, scale),
        out_shape=(
            shape((64, 2 * PLANE), BF16),
            shape((128, 256), BF16),
            shape((n, 64, 128), BF16),
            shape((8, 64, 128), F32),
            shape((27, 64, 128), F32),
        ),
        in_specs=[vmem] * 5,
        out_specs=(vmem,) * 5,
        scratch_shapes=[
            pltpu.VMEM((192, 1152), BF16),
            pltpu.VMEM((256, 256), BF16),
            pltpu.VMEM((2, 128, 256), BF16),
            pltpu.VMEM((n, 64, 128), BF16),
            pltpu.VMEM((4, 64, PLANE), BF16),
            pltpu.VMEM((128, 4 * ROW), BF16),
            pltpu.VMEM((4, 64, PLANE), BF16),
            pltpu.VMEM((192, 4 * ROW), BF16),
            pltpu.VMEM((n, 64, 128), BF16),
            pltpu.VMEM((n, 64, 128), BF16),
            pltpu.VMEM((n * PART, 128), BF16),
            pltpu.VMEM((half, 128), BF16),
            pltpu.VMEM((half, 128), BF16),
            pltpu.VMEM((n // 2, PART, 128), BF16),
            pltpu.VMEM((n * PART, 128), BF16),
            pltpu.SemaphoreType.DMA((6, n)),
            pltpu.SemaphoreType.DMA((6, n)),
        ],
        compiler_params=pltpu.CompilerParams(
            collective_id=0, has_side_effects=True, vmem_limit_bytes=50 * 1024 * 1024
        ),
    )(
        coarse_input.reshape(128, 256),
        skip_rows,
        cotangent.reshape(64, 2 * PLANE),
        w_up,
        w_conv,
    )
    return (
        act.reshape(64, planes, cells),
        grad_in.reshape(128, 1, 256),
        grad_skip.transpose(1, 0, 2).reshape(64, planes * n, 64),
        d_up,
        d_conv,
    )


def solution(mesh):
    body = fused_local if mesh.shape["space"] == 2 * H else local
    in_specs = (
        P("groups", "space", None),
        P("groups", None, "space"),
        P("groups", "space", None),
        P(),
        P(),
    )
    out_specs = (
        P("groups", "space", None),
        P("groups", "space", None),
        P("groups", None, "space"),
        P("groups", None, None),
        P("groups", None, None),
    )
    return jax.shard_map(body, mesh=mesh, in_specs=in_specs, out_specs=out_specs, check_vma=False)
```

```python
import functools
import math

import jax
import jax.numpy as jnp
from jax import lax
from jax.experimental import pallas as pl
from jax.experimental.pallas import tpu as pltpu
from jax.sharding import PartitionSpec as P

W = 128


def padded_2(value, sides, width):
    for axis, dim in sides:
        peers, length = (lax.axis_size(axis), value.shape[dim])
        up = [(i, (i + 1) % peers) for i in range(peers - 1)]
        down = [(j, i) for i, j in up]
        last = lax.slice_in_dim(value, length - width, length, axis=dim)
        leading = lax.slice_in_dim(value, 0, width, axis=dim)
        before = lax.ppermute(last, axis, up)
        after = lax.ppermute(leading, axis, down)
        value = jnp.concatenate([before, value, after], axis=dim)
    return value


def upsample(coarse, w_up, height, width):
    channels = coarse.shape[0]
    planes = coarse.shape[1]
    outputs = w_up.shape[1]
    terms = jnp.dot(
        w_up.reshape(8 * outputs, channels),
        coarse.reshape(channels, -1),
        preferred_element_type=jnp.float32,
    )
    terms = terms.reshape(2, 2, 2, outputs, planes, height // 2, width // 2)
    terms = terms.transpose(3, 4, 0, 5, 1, 6, 2)
    return terms.reshape(outputs, 2 * planes, height, width).astype(jnp.bfloat16)


def pad_sides(volume):
    return jnp.pad(volume, ((0, 0), (0, 0), (1, 1), (1, 1)))


def conv_forward(padded, w_conv, planes, height, width):
    channels = padded.shape[0]
    total = jnp.zeros((w_conv.shape[1], planes * height * width), jnp.float32)
    for depth_tap in range(3):
        for row_tap in range(3):
            for col_tap in range(3):
                window = padded[
                    :,
                    depth_tap : depth_tap + planes,
                    row_tap : row_tap + height,
                    col_tap : col_tap + width,
                ].reshape(channels, -1)
                total = total + jnp.dot(
                    w_conv[9 * depth_tap + 3 * row_tap + col_tap],
                    window,
                    preferred_element_type=jnp.float32,
                )
    return total


def conv_input_grad(padded, w_conv, planes, height, width):
    channels = padded.shape[0]
    total = jnp.zeros((w_conv.shape[2], planes * height * width), jnp.float32)
    for depth_tap in range(3):
        for row_tap in range(3):
            for col_tap in range(3):
                window = padded[
                    :,
                    2 - depth_tap : 2 - depth_tap + planes,
                    2 - row_tap : 2 - row_tap + height,
                    2 - col_tap : 2 - col_tap + width,
                ].reshape(channels, -1)
                total = total + lax.dot_general(
                    w_conv[9 * depth_tap + 3 * row_tap + col_tap],
                    window,
                    (((0,), (0,)), ((), ())),
                    preferred_element_type=jnp.float32,
                )
    return total


def conv_weight_grad(padded, grad_flat, planes, height, width):
    channels = padded.shape[0]
    results = []
    for depth_tap in range(3):
        for row_tap in range(3):
            for col_tap in range(3):
                window = padded[
                    :,
                    depth_tap : depth_tap + planes,
                    row_tap : row_tap + height,
                    col_tap : col_tap + width,
                ].reshape(channels, -1)
                results.append(
                    lax.dot_general(
                        grad_flat,
                        window,
                        (((1,), (1,)), ((), ())),
                        preferred_element_type=jnp.float32,
                    )
                )
    return jnp.stack(results, 0)


def local(coarse_input, skip, cotangent, w_up, w_conv):
    devices = lax.axis_size("space")
    channels_in = coarse_input.shape[0]
    coarse_planes = coarse_input.shape[1]
    up_channels = w_up.shape[1]
    skip_channels = skip.shape[0]
    out_channels = cotangent.shape[0]
    planes = cotangent.shape[1]
    cells = cotangent.shape[2]
    width = W
    height = cells // width
    joined_channels = up_channels + skip_channels
    skip_local = lax.all_to_all(skip, "space", split_axis=1, concat_axis=2, tiled=True)
    upsampled = upsample(coarse_input, w_up, height, width)
    joined = jnp.concatenate([upsampled.reshape(up_channels, planes, cells), skip_local], 0)
    joined_ext = padded_2(joined, (("space", 1),), 1)
    joined_pad = pad_sides(joined_ext.reshape(joined_channels, planes + 2, height, width))
    pre = conv_forward(joined_pad, w_conv, planes, height, width)
    gate = jax.nn.sigmoid(pre)
    activation = (pre * gate).astype(jnp.bfloat16).reshape(out_channels, planes, cells)
    grad_pre = (
        cotangent.reshape(out_channels, -1).astype(jnp.float32) * gate * (1.0 + pre * (1.0 - gate))
    ).astype(jnp.bfloat16)
    grad_ext = padded_2(grad_pre.reshape(out_channels, planes, cells), (("space", 1),), 1)
    grad_pad = pad_sides(grad_ext.reshape(out_channels, planes + 2, height, width))
    grad_joined = conv_input_grad(grad_pad, w_conv, planes, height, width)
    grad_up = grad_joined[:up_channels].astype(jnp.bfloat16)
    skip_part = grad_joined[up_channels:].astype(jnp.bfloat16).reshape(skip_channels, planes, cells)
    grad_skip = lax.all_to_all(skip_part, "space", split_axis=2, concat_axis=1, tiled=True)
    arranged = (
        grad_up.reshape(up_channels, coarse_planes, 2, height // 2, 2, width // 2, 2)
        .transpose(2, 4, 6, 0, 1, 3, 5)
        .reshape(8 * up_channels, -1)
    )
    flat_up = w_up.reshape(8 * up_channels, channels_in)
    grad_input = lax.dot_general(
        flat_up, arranged, (((0,), (0,)), ((), ())), preferred_element_type=jnp.float32
    )
    grad_input = grad_input.astype(jnp.bfloat16).reshape(channels_in, coarse_planes, -1)
    local_up = lax.dot_general(
        arranged,
        coarse_input.reshape(channels_in, -1),
        (((1,), (1,)), ((), ())),
        preferred_element_type=jnp.float32,
    )
    local_up = local_up.reshape(8, up_channels, channels_in)
    local_conv = conv_weight_grad(joined_pad, grad_pre, planes, height, width)
    scale = 1.0 / math.sqrt(devices * planes * cells)
    summed_up, summed_conv = lax.psum((local_up * scale, local_conv * scale), "space")
    return (activation, grad_input, grad_skip, summed_up, summed_conv)


H = 8
ROW = (H + 2) * W
PLANE = H * W
CONV_PART = 112
UP_PART = 32
F32 = jnp.float32
BF16 = jnp.bfloat16


def remote(src, dst, send, recv, peer):
    return pltpu.make_async_remote_copy(
        src_ref=src,
        dst_ref=dst,
        send_sem=send,
        recv_sem=recv,
        device_id={"space": peer},
        device_id_type=pl.DeviceIdType.MESH,
    )


def mm(a, b):
    return jnp.dot(a, b, preferred_element_type=F32)


def mm_nt(a, b):
    return lax.dot_general(a, b, (((1,), (1,)), ((), ())), preferred_element_type=F32)


def mm_tn(a, b):
    return lax.dot_general(a, b, (((0,), (0,)), ((), ())), preferred_element_type=F32)


class Reducer:
    def __init__(self, me, n, scale, size, part, pair, total, got, full, send, recv, sem):
        self.chips, self.core, self.chip = n // 2, lax.rem(me, 2), lax.div(me, 2)
        self.scale, self.size, self.half = scale, size, n // 2 * size
        self.part, self.pair, self.total, self.got, self.full = part, pair, total, got, full
        self.send, self.recv, self.sem = send, recv, sem
        self.partner = me + 1 - 2 * self.core
        self.mine = pl.ds(pl.multiple_of(self.core * self.half, 16), self.half)
        self.other = pl.ds(pl.multiple_of((1 - self.core) * self.half, 16), self.half)
        self.own = pl.ds(pl.multiple_of(self.core * self.half + self.chip * size, 16), size)

    def chunk(self, index):
        return pl.ds(pl.multiple_of(index * self.size, 16), self.size)

    def swap(self):
        s = self.sem
        return remote(self.part.at[self.other], self.pair, self.send.at[s, 0], self.recv.at[s, 0], self.partner)

    def reduce_copy(self, k):
        peer, s = lax.rem(self.chip + k, self.chips), self.sem
        return remote(
            self.total.at[self.chunk(peer)], self.got.at[k], self.send.at[s, k], self.recv.at[s, k],
            2 * peer + self.core,
        )

    def gather_copy(self, k):
        peer, s = lax.rem(self.chip + k, self.chips), self.sem + 1
        return remote(
            self.full.at[self.own], self.full.at[self.own], self.send.at[s, k], self.recv.at[s, k],
            2 * peer + self.core,
        )

    def back(self):
        s = self.sem + 1
        return remote(
            self.full.at[self.mine], self.full.at[self.mine], self.send.at[s, 0], self.recv.at[s, 0], self.partner
        )

    def start_swap(self):
        self.swap().start()

    def start_reduce(self):
        self.swap().wait()
        self.total[...] = (self.part[self.mine, :].astype(F32) + self.pair[...].astype(F32)).astype(BF16)

        @pl.loop(1, self.chips)
        def _(k):
            self.reduce_copy(k).start()

    def start_gather(self):
        @pl.loop(1, self.chips)
        def _(k):
            self.reduce_copy(k).wait()

        summed = self.total[self.chunk(self.chip), :].astype(F32)
        for k in range(1, self.chips):
            summed = summed + self.got[k].astype(F32)
        self.full[self.own, :] = (summed * self.scale).astype(BF16)

        @pl.loop(1, self.chips)
        def _(k):
            self.gather_copy(k).start()

    def start_back(self):
        @pl.loop(1, self.chips)
        def _(k):
            self.gather_copy(k).wait()

        self.back().start()

    def wait_back(self):
        self.back().wait()


def fused_kernel(
    n, scale,
    coarse, skip, cot, w_up, w_conv,
    act_out, gin_out, gskip_out, gup_out, gconv_out,
    w_s, w_u, y_buf, c_halo, s_got, s_planes, x_buf, g_planes, g_buf, t_send, t_got,
    part, pair, total, got, full, u_part, u_pair, u_total, u_got, u_full, send, recv,
):
    me = lax.axis_index("space")
    lane = lax.broadcasted_iota(jnp.int32, (64, W), 1)
    low = lane < 64

    c_halo[...] = jnp.zeros_like(c_halo)
    for plane in (0, 3):
        s_planes[plane] = jnp.zeros((64, PLANE), BF16)
        g_planes[plane] = jnp.zeros((64, PLANE), BF16)

    barrier = pltpu.get_barrier_semaphore()

    @pl.loop(1, n)
    def _(k):
        pl.semaphore_signal(
            barrier, inc=1, device_id={"space": lax.rem(me + k, n)},
            device_id_type=pl.DeviceIdType.MESH,
        )

    pl.semaphore_wait(barrier, n - 1)

    def skip_copy(k):
        peer = lax.rem(me + k, n)
        return remote(skip.at[peer], s_got.at[me], send.at[0, k], recv.at[0, k], peer)

    @pl.loop(1, n)
    def _(k):
        skip_copy(k).start()

    def halo(src_up, src_down, dst_prev, dst_next, index):
        up = remote(src_up, dst_prev, send.at[1, index], recv.at[1, index], me + 1)
        down = remote(src_down, dst_next, send.at[1, index + 1], recv.at[1, index + 1], me - 1)

        def start():
            pl.when(me < n - 1)(up.start)
            pl.when(me > 0)(down.start)

        def wait():
            pl.when(me < n - 1)(up.wait_send)
            pl.when(me > 0)(down.wait_send)
            pl.when(me > 0)(up.wait_recv)
            pl.when(me < n - 1)(down.wait_recv)

        return start, wait

    c_start, c_wait = halo(coarse, coarse, c_halo.at[0], c_halo.at[1], 0)
    c_start()

    x_buf[...] = jnp.zeros_like(x_buf)
    g_buf[...] = jnp.zeros_like(g_buf)
    for a in range(3):
        for c in range(3):
            rows = slice(64 * c, 64 * c + 64)
            t0, t1, t2 = [w_conv[9 * a + 3 * b + c].astype(F32) for b in range(3)]
            w_s[a, rows, 0:128] = jnp.where(low, t0, pltpu.roll(t1, 64, 1)).astype(BF16)
            w_s[a, rows, 128:256] = t2.astype(BF16)
            w_s[3 + a, rows, 0:128] = jnp.where(low, pltpu.roll(t0, 64, 1), t1).astype(BF16)
            w_s[3 + a, rows, 128:256] = pltpu.roll(t2, 64, 1).astype(BF16)
    for ij in range(4):
        for k in range(2):
            w_u[64 * ij : 64 * ij + 64, 128 * k : 128 * k + 128] = w_up[2 * ij + k]

    source = lax.broadcasted_iota(jnp.int32, (W, W), 0)
    target = lax.broadcasted_iota(jnp.int32, (W, W), 1)

    def spread(h2, k):
        return jnp.where(target == 2 * (source - 64 * h2) + k, 1.0, 0.0).astype(BF16)

    spreads = [[jnp.where((source >= 64 * h2) & (source < 64 * h2 + 64), spread(h2, k), 0) for k in range(2)] for h2 in range(2)]

    def expand(value):
        return jnp.concatenate(
            [
                jnp.concatenate(
                    [mm(value[:, 128 * (h // 2) : 128 * (h // 2) + 128], spreads[h % 2][k]) for h in range(H // 2)],
                    axis=1,
                )
                for k in range(2)
            ],
            axis=0,
        ).astype(BF16)

    def place(value, plane, j):
        for h in range(H // 2):
            at = plane * ROW + (2 * h + j + 1) * W
            x_buf[0:64, at : at + W] = value[:, h * W : (h + 1) * W].astype(BF16)

    c_exp = expand(coarse[...])
    up = mm(w_u[...], c_exp)
    for ij in range(4):
        place(up[64 * ij : 64 * ij + 64], 1 + ij // 2, ij % 2)
    c_wait()
    up = mm(w_u[128:256], expand(c_halo[0]))
    place(up[0:64], 0, 0)
    place(up[64:128], 0, 1)
    up = mm(w_u[0:128], expand(c_halo[1]))
    place(up[0:64], 3, 0)
    place(up[64:128], 3, 1)

    def forward(side, plane, a):
        parts = []
        for b in range(3):
            at = (plane + a) * ROW + b * W
            parts.append(x_buf[64 * side : 64 * side + 64, at : at + PLANE])
        return mm(w_s[3 * side + a, :, 0:192], jnp.concatenate(parts, axis=0))

    for plane in range(2):
        y_buf[plane] = forward(0, plane, 0) + forward(0, plane, 1) + forward(0, plane, 2)

    @pl.loop(1, n)
    def _(k):
        skip_copy(k).wait()

    s_got[me] = skip[me]
    for h in range(H):
        left = s_got[2 * h].astype(F32)
        right = s_got[2 * h + 1].astype(F32)
        first = jnp.where(low, left, pltpu.roll(right, 64, 1)).astype(BF16)
        second = jnp.where(low, pltpu.roll(left, 64, 1), right).astype(BF16)
        s_planes[1, :, h * W : (h + 1) * W] = first
        s_planes[2, :, h * W : (h + 1) * W] = second
    s_start, s_wait = halo(s_planes.at[2], s_planes.at[1], s_planes.at[0], s_planes.at[3], 2)
    s_start()
    for plane in (1, 2):
        x_buf[64:128, plane * ROW + W : plane * ROW + W + PLANE] = s_planes[plane]
    for plane in range(2):
        y_buf[plane] = y_buf[plane] + (forward(1, plane, 1) + forward(1, plane, 2 - 2 * plane))
    s_wait()
    for plane in (0, 3):
        x_buf[64:128, plane * ROW + W : plane * ROW + W + PLANE] = s_planes[plane]

    def windows(buf, plane, sign):
        parts = []
        for a in range(3):
            for b in range(3):
                at = (plane + 1 + sign * (a - 1)) * ROW + W + sign * (b - 1) * W
                parts.append(buf[:, at : at + PLANE])
        return jnp.concatenate(parts, axis=0)

    for plane in range(2):
        y = y_buf[plane] + forward(1, plane, 2 * plane)
        for h in range(H):
            at = slice(h * W, (h + 1) * W)
            full_at = slice(plane * PLANE + h * W, plane * PLANE + (h + 1) * W)
            pre = (
                y[64:128, at]
                + jnp.where(lane > 0, pltpu.roll(y[0:64, at], 1, 1), 0.0)
                + jnp.where(lane < W - 1, pltpu.roll(y[128:192, at], W - 1, 1), 0.0)
            )
            gate = 1.0 / (1.0 + jnp.exp(-pre))
            act_out[:, full_at] = (pre * gate).astype(BF16)
            grad = cot[:, full_at].astype(F32) * gate * (1.0 + pre * (1.0 - gate))
            g_planes[plane + 1, :, at] = grad.astype(BF16)

    g_start, g_wait = halo(g_planes.at[2], g_planes.at[1], g_planes.at[0], g_planes.at[3], 4)
    g_start()

    def fill(plane):
        for h in range(H):
            value = g_planes[plane, :, h * W : (h + 1) * W]
            wide = value.astype(F32)
            at = plane * ROW + (h + 1) * W
            g_buf[64:128, at : at + W] = value
            g_buf[0:64, at : at + W] = jnp.where(lane < W - 1, pltpu.roll(wide, W - 1, 1), 0.0).astype(BF16)
            g_buf[128:192, at : at + W] = jnp.where(lane > 0, pltpu.roll(wide, 1, 1), 0.0).astype(BF16)

    fill(1)
    fill(2)

    d_conv = None
    for plane in range(2):
        at = (plane + 1) * ROW + W
        term = mm_nt(g_buf[:, at : at + PLANE], windows(x_buf, plane, 1))
        d_conv = term if d_conv is None else d_conv + term
    for a in range(3):
        for b in range(3):
            for c in range(3):
                ab = 3 * a + b
                row = 64 * (9 * a + 3 * b + c)
                part[row : row + 64, :] = d_conv[64 * c : 64 * c + 64, 128 * ab : 128 * ab + 128].astype(BF16)

    part[27 * 64 :, :] = jnp.zeros((n * CONV_PART - 27 * 64, 128), BF16)
    conv_sum = Reducer(me, n, scale, CONV_PART, part, pair, total, got, full, send, recv, 3)
    up_sum = Reducer(me, n, scale, UP_PART, u_part, u_pair, u_total, u_got, u_full, send, recv, 5)
    conv_sum.start_swap()

    g_wait()
    fill(0)
    fill(3)
    w_b = w_conv[...].reshape(27 * 64, 128)
    joined = [mm_tn(w_b, windows(g_buf, 0, -1))]
    conv_sum.start_reduce()
    joined.append(mm_tn(w_b, windows(g_buf, 1, -1)))
    for h in range(H):
        at = slice(h * W, (h + 1) * W)
        first, second = joined[0][64:128, at], joined[1][64:128, at]
        t_send[2 * h] = jnp.where(low, first, pltpu.roll(second, 64, 1)).astype(BF16)
        t_send[2 * h + 1] = jnp.where(low, pltpu.roll(first, 64, 1), second).astype(BF16)

    def grad_copy(k):
        peer = lax.rem(me + k, n)
        return remote(t_send.at[peer], t_got.at[me], send.at[2, k], recv.at[2, k], peer)

    @pl.loop(1, n)
    def _(k):
        grad_copy(k).start()

    g_up = jnp.concatenate(
        [
            jnp.concatenate([joined[ij // 2][0:64, (2 * h + ij % 2) * W : (2 * h + ij % 2 + 1) * W] for h in range(H // 2)], axis=1)
            for ij in range(4)
        ],
        axis=0,
    ).astype(BF16)
    d_up = mm_nt(g_up, c_exp)
    for ij in range(4):
        for k in range(2):
            row = 64 * (2 * ij + k)
            u_part[row : row + 64, :] = d_up[64 * ij : 64 * ij + 64, 128 * k : 128 * k + 128].astype(BF16)
    up_sum.start_swap()

    squeeze = jnp.where(source == 2 * lax.rem(target, 64) + lax.div(target, 64), 1.0, 0.0).astype(BF16)
    wide_low = lax.broadcasted_iota(jnp.int32, (128, W), 1) < 64
    packed = [mm(g_up[:, h * W : (h + 1) * W], squeeze).astype(BF16) for h in range(H // 2)]
    both = mm_tn(w_u[...], jnp.concatenate(packed, axis=1))
    for h in range(0, H // 2, 2):
        z0 = both[0:128, h * W : (h + 1) * W] + pltpu.roll(both[128:256, h * W : (h + 1) * W], 64, 1)
        z1 = pltpu.roll(both[0:128, (h + 1) * W : (h + 2) * W], 64, 1) + both[128:256, (h + 1) * W : (h + 2) * W]
        gin_out[:, h * 64 : h * 64 + 128] = jnp.where(wide_low, z0, z1).astype(BF16)

    conv_sum.start_gather()
    up_sum.start_reduce()
    up_sum.start_gather()

    @pl.loop(1, n)
    def _(k):
        grad_copy(k).wait()

    t_got[me] = t_send[me]
    gskip_out[...] = t_got[...]

    conv_sum.start_back()
    up_sum.start_back()
    conv_sum.wait_back()
    up_sum.wait_back()
    for tap in range(27):
        gconv_out[tap] = full[64 * tap : 64 * tap + 64, :].astype(F32)
    for tap in range(8):
        gup_out[tap] = u_full[64 * tap : 64 * tap + 64, :].astype(F32)


def fused_local(coarse_input, skip, cotangent, w_up, w_conv):
    n = lax.axis_size("space")
    planes = cotangent.shape[1]
    cells = cotangent.shape[2]
    skip_rows = skip.reshape(64, n, 128).transpose(1, 0, 2)
    scale = 1.0 / math.sqrt(n * planes * cells)
    shape = jax.ShapeDtypeStruct
    vmem = pl.BlockSpec(memory_space=pltpu.VMEM)
    act, grad_in, grad_skip, d_up, d_conv = pl.pallas_call(
        functools.partial(fused_kernel, n, scale),
        out_shape=(
            shape((64, 2 * PLANE), BF16),
            shape((128, 256), BF16),
            shape((n, 64, 128), BF16),
            shape((8, 64, 128), F32),
            shape((27, 64, 128), F32),
        ),
        in_specs=[vmem] * 5,
        out_specs=(vmem,) * 5,
        scratch_shapes=[
            pltpu.VMEM((6, 192, 256), BF16),
            pltpu.VMEM((256, 256), BF16),
            pltpu.VMEM((2, 192, PLANE), F32),
            pltpu.VMEM((2, 128, 256), BF16),
            pltpu.VMEM((n, 64, 128), BF16),
            pltpu.VMEM((4, 64, PLANE), BF16),
            pltpu.VMEM((128, 4 * ROW), BF16),
            pltpu.VMEM((4, 64, PLANE), BF16),
            pltpu.VMEM((192, 4 * ROW), BF16),
            pltpu.VMEM((n, 64, 128), BF16),
            pltpu.VMEM((n, 64, 128), BF16),
            pltpu.VMEM((n * CONV_PART, 128), BF16),
            pltpu.VMEM((n // 2 * CONV_PART, 128), BF16),
            pltpu.VMEM((n // 2 * CONV_PART, 128), BF16),
            pltpu.VMEM((n // 2, CONV_PART, 128), BF16),
            pltpu.VMEM((n * CONV_PART, 128), BF16),
            pltpu.VMEM((n * UP_PART, 128), BF16),
            pltpu.VMEM((n // 2 * UP_PART, 128), BF16),
            pltpu.VMEM((n // 2 * UP_PART, 128), BF16),
            pltpu.VMEM((n // 2, UP_PART, 128), BF16),
            pltpu.VMEM((n * UP_PART, 128), BF16),
            pltpu.SemaphoreType.DMA((7, n)),
            pltpu.SemaphoreType.DMA((7, n)),
        ],
        compiler_params=pltpu.CompilerParams(
            collective_id=0, has_side_effects=True, vmem_limit_bytes=50 * 1024 * 1024
        ),
    )(
        coarse_input.reshape(128, 256),
        skip_rows,
        cotangent.reshape(64, 2 * PLANE),
        w_up,
        w_conv,
    )
    return (
        act.reshape(64, planes, cells),
        grad_in.reshape(128, 1, 256),
        grad_skip.transpose(1, 0, 2).reshape(64, planes * n, 64),
        d_up,
        d_conv,
    )


def solution(mesh):
    body = fused_local if mesh.shape["space"] == 2 * H else local
    in_specs = (
        P("groups", "space", None),
        P("groups", None, "space"),
        P("groups", "space", None),
        P(),
        P(),
    )
    out_specs = (
        P("groups", "space", None),
        P("groups", "space", None),
        P("groups", None, "space"),
        P("groups", None, None),
        P("groups", None, None),
    )
    return jax.shard_map(body, mesh=mesh, in_specs=in_specs, out_specs=out_specs, check_vma=False)
```
